256 devices in a mesh: section: 2 (over core), dp: 8 (over x, y_lo), tensor: 16 (over z, y_hi).
Axes of the slice: x: 4, y: 4 (y_hi: 2, y_lo: 2; y = y_hi * 2 + y_lo), z: 8, core: 2. Of those that a mesh axis runs over, the one named last changes fastest.
Arguments:
- layer_inputs: bfloat16 [2, 1024, 9216], P('section', 'tensor', 'dp'), may hold values from -0.75 to 0.75
- projection: bfloat16 [2, 9216, 36864], P('section', 'dp', 'tensor'), may hold values from -0.0625 to 0.0625
- pre_act: bfloat16 [2, 1024, 36864], P('section', 'dp', 'tensor'), may hold values from -6 to 6
- act_grad: bfloat16 [2, 1024, 36864], P('section', 'dp', 'tensor'), may hold values from -2 to 2
Outputs:
- weight_grad: bfloat16 [2, 9216, 36864], P('section', 'dp', 'tensor')
- prev_grad: bfloat16 [2, 1024, 9216], P('section', 'tensor', 'dp')
The draws below stay inside these ranges and needn't reach their ends.
All inputs are finite; a program needn't handle non-finite values.
Results may differ from the reference program's by a relative error of at most 0.019.
Values may be sent and summed in bfloat16 or wider, within the bound.
No kernel may reach another device: no remote copies, remote signals or barrier semaphores. Data moves between devices by JAX's collectives and lax.ppermute only.
A program may use at most 64 MiB of HBM per device.

```python
import jax
import jax.numpy as jnp
from jax import lax

D = 9216
F = 36864
TOKENS = 1024
SECTIONS = 2
N_TENSOR = 16


def block_scale(stream_key, extent, cuts, least, high):
    gain = 1.0
    for position, parts in cuts:
        heights = jax.random.uniform(jax.random.fold_in(jax.random.fold_in(stream_key, 6), position), (parts,), jnp.float32, least / len(cuts), high / len(cuts))
        gain = gain * jnp.repeat(jnp.exp(heights), extent[position] // parts).reshape((-1,) + (1,) * (len(extent) - 1 - position))
    return gain


def bell_draw(key, dims, scale, reach, split=(), kind=jnp.bfloat16):
    result = jax.random.normal(key, dims, jnp.float32) * scale
    if len(split) > 0:
        result = block_scale(key, dims, split, -0.22, 0.18) * result
    return jnp.clip(result, min=-reach, max=reach).astype(kind)


def setup_inputs(seed: int = 0) -> dict:
    key_list = jax.random.split(jax.random.key(seed), 5)
    layer_inputs = bell_draw(key_list[0], (SECTIONS, TOKENS, D), (4.0 * TOKENS ** -0.5), 0.75, ((0, 2), (1, 16), (2, 8)))
    projection = bell_draw(key_list[1], (SECTIONS, D, F), D ** -0.5, 0.0625, ((0, 2), (1, 8), (2, 16)))
    pre_act = bell_draw(key_list[2], (SECTIONS, TOKENS, F), 1.0, 6.0, ((0, 2), (1, 8), (2, 16)))
    act_grad = bell_draw(key_list[3], (SECTIONS, TOKENS, F), 0.35, 2.0, ((0, 2), (1, 8), (2, 16)))
    return dict(layer_inputs=layer_inputs, projection=projection, pre_act=pre_act, act_grad=act_grad)


def block_sum(pre_grad, weight):
    width = pre_grad.shape[1] // N_TENSOR
    grad_blocks = pre_grad.reshape(pre_grad.shape[0], N_TENSOR, width).transpose(1, 0, 2)
    weight_blocks = weight.reshape(weight.shape[0], N_TENSOR, width).transpose(1, 0, 2)

    def add_block(total, pair):
        grad_part, weight_part = pair
        term = lax.dot_general(grad_part, weight_part, (((1,), (1,)), ((), ())), preferred_element_type=jnp.float32)
        rounded = lax.optimization_barrier(term.astype(jnp.bfloat16))
        return total + rounded.astype(jnp.float32), None

    start = jnp.zeros((pre_grad.shape[0], weight.shape[0]), jnp.float32)
    total, _ = lax.scan(add_block, start, (grad_blocks, weight_blocks))
    return total


def reference(layer_inputs, projection, pre_act, act_grad):
    weight_grads = []
    layer_grads = []
    for section in range(SECTIONS):
        pre_grad = (2.0 * jnp.maximum(pre_act[section].astype(jnp.float32), 0.0) * act_grad[section].astype(jnp.float32)).astype(jnp.bfloat16)
        weight_grads.append(jnp.dot(layer_inputs[section].T, pre_grad, preferred_element_type=jnp.float32).astype(jnp.bfloat16))
        layer_grads.append(block_sum(pre_grad, projection[section]).astype(jnp.bfloat16))
    weight_grad = jnp.stack(weight_grads)
    layer_grad = jnp.stack(layer_grads)
    return weight_grad, jnp.roll(layer_grad, -1, axis=0)
```

```python
import jax
import jax.numpy as jnp
from jax import lax
from jax.sharding import PartitionSpec as P

F32, BF16 = jnp.float32, jnp.bfloat16


def shift(block, axis, distance):
    n = lax.axis_size(axis)
    return lax.ppermute(block, axis, [(i, (i + distance) % n) for i in range(n)])


def swap(block, axis):
    n = lax.axis_size(axis)
    return lax.ppermute(block, axis, [(i, i ^ 1) for i in range(n)])


def gather_inputs(own, z_size, y_hi):
    other = swap(own, "tensor")
    pair = jnp.where(y_hi == 0, jnp.concatenate([own, other]), jnp.concatenate([other, own]))
    half = own.shape[0]
    got = {0: pair}
    up, down = pair, pair
    for step in range(1, z_size // 2):
        up = shift(up, "tensor", 2)
        down = shift(down, "tensor", -2)
        got[z_size - step] = up
        got[step] = down
    far_up = shift(up[:half], "tensor", 2)
    far_down = shift(down[half:], "tensor", -2)
    got[z_size // 2] = jnp.concatenate([far_up, far_down])
    return jnp.concatenate([got[i] for i in range(z_size)])


def on_device(layer_inputs, projection, pre_act, act_grad):
    weight = projection[0]
    dp, tensor = lax.axis_index("dp"), lax.axis_index("tensor")
    x, y_lo, z, y_hi = dp // 2, dp % 2, tensor // 2, tensor % 2
    rows = pre_act.shape[1]
    half = rows // 2
    wide = pre_act.shape[2]
    third = wide // 3

    own = (
        2.0 * jnp.maximum(pre_act[0].astype(F32), 0.0) * act_grad[0].astype(F32)
    ).astype(BF16)

    inputs = gather_inputs(layer_inputs[0], 8, y_hi)

    left = shift(own, "dp", 2)
    right = shift(own, "dp", -2)
    beside = swap(own, "dp")
    from_left = shift(jnp.concatenate([left[:half], beside[:half]]), "dp", 2)
    from_right = shift(jnp.concatenate([right[half:], beside[:half]]), "dp", -2)
    from_beside = swap(jnp.concatenate([left[half:], right[half:]]), "dp")
    across = jnp.concatenate([from_left[:half], from_right[:half]])
    left_beside = jnp.concatenate([from_left[half:], from_beside[:half]])
    right_beside = jnp.concatenate([from_right[half:], from_beside[half:]])
    far = jnp.concatenate(
        [
            shift(left_beside[:, :third], "dp", 2),
            shift(right_beside[:, third : 2 * third], "dp", -2),
            swap(across[:, 2 * third :], "dp"),
        ],
        axis=1,
    )
    order = [
        ((0, 0), own),
        ((0, 1), beside),
        ((1, 0), right),
        ((3, 0), left),
        ((1, 1), right_beside),
        ((2, 0), across),
        ((3, 1), left_beside),
        ((2, 1), far),
    ]
    partial = jnp.zeros((8 * rows, weight.shape[0]), BF16)
    places = []
    for (dx, dy), block in order:
        place = ((x + dx) % 4) * 2 + (y_lo ^ dy)
        places.append(place)
        part = lax.dot_general(block, weight, (((1,), (1,)), ((), ())), preferred_element_type=F32)
        partial = lax.dynamic_update_slice(partial, part.astype(BF16), (place * rows, 0))

    def part_of(offset, start=0, size=rows):
        where = ((z + offset) % 8) * rows + start
        return lax.dynamic_slice(partial, (where, 0), (size, partial.shape[1])).astype(F32)

    up = shift(part_of(4, 0, half).astype(BF16), "tensor", 2)
    down = shift(part_of(4, half, half).astype(BF16), "tensor", -2)
    up = jnp.concatenate([part_of(3, 0, half) + up.astype(F32), part_of(3, half, half)])
    down = jnp.concatenate([part_of(-3, 0, half), part_of(-3, half, half) + down.astype(F32)])
    up = shift(up.astype(BF16), "tensor", 2)
    down = shift(down.astype(BF16), "tensor", -2)
    for offset in (2, 1):
        up = shift((part_of(offset) + up.astype(F32)).astype(BF16), "tensor", 2)
        down = shift((part_of(-offset) + down.astype(F32)).astype(BF16), "tensor", -2)
    total = part_of(0) + up.astype(F32) + down.astype(F32)
    mine = lax.dynamic_slice(total, (y_hi * half, 0), (half, total.shape[1])).astype(BF16)
    theirs = lax.dynamic_slice(total, ((1 - y_hi) * half, 0), (half, total.shape[1])).astype(BF16)
    near = lax.ppermute(mine, "section", [(0, 1), (1, 0)])
    across_pair = [
        (s * 16 + t, (1 - s) * 16 + (t ^ 1)) for s in range(2) for t in range(16)
    ]
    away = lax.ppermute(theirs, ("section", "tensor"), across_pair)
    handed = (near.astype(F32) + away.astype(F32)).astype(BF16)

    grads = jnp.concatenate([block for _, block in order])
    matched = jnp.concatenate(
        [
            lax.dynamic_slice(inputs, (((place - z) % 8) * rows, 0), (rows, inputs.shape[1]))
            for place in places
        ]
    )
    weight_grad = lax.dot_general(
        matched, grads, (((0,), (0,)), ((), ())), preferred_element_type=F32
    ).astype(BF16)
    return (weight_grad[None], handed[None])


def solution(mesh):
    return jax.shard_map(
        on_device,
        mesh=mesh,
        in_specs=(
            P("section", "tensor", "dp"),
            P("section", "dp", "tensor"),
            P("section", "dp", "tensor"),
            P("section", "dp", "tensor"),
        ),
        out_specs=(P("section", "dp", "tensor"), P("section", "tensor", "dp")),
        check_vma=False,
    )
```

```python
import jax
import jax.numpy as jnp
from jax import lax
from jax.experimental import pallas as pl
from jax.experimental.pallas import tpu as pltpu
from jax.sharding import PartitionSpec as P

F32, BF16 = jnp.float32, jnp.bfloat16
Z, DP, T, S = 8, 8, 16, 2
together = lax.optimization_barrier
OVER_LAST = (((1,), (1,)), ((), ()))


def shift(block, axis, distance):
    n = lax.axis_size(axis)
    return lax.ppermute(block, axis, [(i, (i + distance) % n) for i in range(n)])


def swap(block, axis):
    n = lax.axis_size(axis)
    return lax.ppermute(block, axis, [(i, i ^ 1) for i in range(n)])


def along_z(blocks, distance):
    route = []
    for s in range(S):
        for t in range(T):
            to = (t + 2 * (distance if s == 0 else -distance)) % T
            route.append((s * T + t, s * T + to))
    return lax.ppermute(blocks, ("section", "tensor"), route)


def deliver(block, dz, flip):
    route = []
    for s in range(S):
        for t in range(T):
            to = ((t // 2 + dz) % Z) * 2 + (t % 2 ^ flip)
            route.append((s * T + t, (1 - s) * T + to))
    return lax.ppermute(block, ("section", "tensor"), route)


def times_kernel(block_ref, weight_ref, out_ref):
    wide = weight_ref.shape[0]
    for start in range(0, wide, 256):
        stop = min(start + 256, wide)
        out_ref[:, start:stop] = lax.dot_general(
            block_ref[...],
            weight_ref[start:stop, :],
            (((1,), (1,)), ((), ())),
            preferred_element_type=F32,
        ).astype(out_ref.dtype)


def times(block, weight):
    rows, depth = block.shape
    wide = weight.shape[0]
    return pl.pallas_call(
        times_kernel,
        in_specs=[pl.BlockSpec(memory_space=pltpu.VMEM)] * 2,
        out_specs=pl.BlockSpec(memory_space=pltpu.VMEM),
        out_shape=jax.ShapeDtypeStruct((rows, wide), BF16),
        cost_estimate=pl.CostEstimate(
            flops=2 * rows * depth * wide,
            bytes_accessed=2 * (rows * depth + wide * depth + rows * wide),
            transcendentals=0,
        ),
        compiler_params=pltpu.CompilerParams(vmem_limit_bytes=8 * 2**20),
        name="times",
    )(block, weight)


def place(dx, dy):
    dp = lax.axis_index("dp")
    return ((dp // 2 + dx) % 4) * 2 + (dp % 2 + dy) % 2


FIRST = ((0, 0), (0, 1), (1, 0), (3, 0))
SECOND = ((1, 1), (2, 0), (3, 1))
FAR = ((2, 1),)


def far_kernel(first_ref, second_ref, left_ref, right_ref, weight_ref, out_ref):
    tensor = lax.axis_index("tensor")
    z, y_hi = tensor // 2, tensor % 2
    rows, middle = left_ref.shape
    half = rows // 2

    def fill(which, source, index, columns=slice(None)):
        block = ((place(*which) - z + Z) % Z) * rows
        for high in range(2):
            away = y_hi if high == 0 else 1 - y_hi
            where = pl.multiple_of(block + away * half, half)
            begin = index * rows + high * half
            out_ref[pl.ds(where, half), columns] = source[begin : begin + half, :]

    for i, which in enumerate(FIRST):
        fill(which, first_ref, i)
    for i, which in enumerate(SECOND):
        fill(which, second_ref, i)
    wide = weight_ref.shape[0]
    for start in range(0, wide, 256):
        some = slice(start, min(start + 256, wide))
        total = lax.dot_general(
            left_ref[...], weight_ref[some, :middle], OVER_LAST, preferred_element_type=F32
        )
        total += lax.dot_general(
            right_ref[...], weight_ref[some, middle:], OVER_LAST, preferred_element_type=F32
        )
        fill(FAR[0], total.astype(out_ref.dtype), 0, some)


def all_terms(first, second, left, right, weight):
    rows, middle = left.shape
    wide = weight.shape[0]
    return pl.pallas_call(
        far_kernel,
        in_specs=[pl.BlockSpec(memory_space=pltpu.VMEM)] * 5,
        out_specs=pl.BlockSpec(memory_space=pltpu.VMEM),
        out_shape=jax.ShapeDtypeStruct((DP * rows, wide), BF16),
        cost_estimate=pl.CostEstimate(
            flops=4 * rows * middle * wide,
            bytes_accessed=2 * (2 * rows * middle + 2 * wide * middle + 2 * DP * rows * wide),
            transcendentals=0,
        ),
        compiler_params=pltpu.CompilerParams(vmem_limit_bytes=8 * 2**20),
        name="all_terms",
    )(first, second, left, right, weight)


def weight_kernel(*refs):
    blocks, pieces = refs[:9], refs[9:15]
    out_ref, token_ref, grads, inputs = refs[15:]
    own, beside, right, left, from_left, from_right, from_beside, far_left, far_right = blocks
    half = own.shape[0] // 2
    middle = far_left.shape[1]
    step = out_ref.shape[0]

    @pl.when(pl.program_id(0) == 0)
    def _():
        tensor, section = lax.axis_index("tensor"), lax.axis_index("section")
        z, y_hi = tensor // 2, tensor % 2
        token_ref[...] = jnp.zeros_like(token_ref)

        def fill(spot, high, source, part, columns=slice(None)):
            apart = z - place(*(FIRST + SECOND + FAR)[spot])
            order = (apart * (1 - 2 * section) + Z) % Z
            away = y_hi if high == 0 else 1 - y_hi
            where = pl.multiple_of((order + away * Z) * half, half)
            grads[pl.ds(where, half), columns] = source[part * half : (part + 1) * half, :]

        for spot, block in enumerate((own, beside, right, left)):
            fill(spot, 0, block, 0)
            fill(spot, 1, block, 1)
        fill(4, 0, from_right, 1)
        fill(4, 1, from_beside, 1)
        fill(5, 0, from_left, 0)
        fill(5, 1, from_right, 0)
        fill(6, 0, from_left, 1)
        fill(6, 1, from_beside, 0)
        for block, columns in ((far_left, slice(0, middle)), (far_right, slice(middle, None))):
            fill(7, 0, block, 0, columns)
            fill(7, 1, block, 1, columns)
        start = 0
        for block in pieces:
            inputs[start : start + block.shape[0], :] = block[...]
            start += block.shape[0]

    columns = pl.ds(pl.multiple_of(pl.program_id(0) * step, step), step)
    part = inputs[:, columns].T
    wide = grads.shape[1]
    for start in range(0, wide, wide // 3):
        some = slice(start, start + wide // 3)
        out_ref[:, some] = jnp.dot(
            part, grads[:, some], preferred_element_type=F32
        ).astype(out_ref.dtype)


def weight_times(blocks, inputs):
    rows, depth = 8 * blocks[0].shape[0], blocks[0].shape[1]
    wide = inputs[0].shape[1]
    step = wide // 3
    return pl.pallas_call(
        weight_kernel,
        grid=(wide // step,),
        in_specs=[pl.BlockSpec(memory_space=pltpu.VMEM)] * (len(blocks) + len(inputs)),
        out_specs=(
            pl.BlockSpec((step, depth), lambda i: (i, 0)),
            pl.BlockSpec((8, 128), lambda i: (0, 0)),
        ),
        out_shape=(
            jax.ShapeDtypeStruct((wide, depth), BF16),
            jax.ShapeDtypeStruct((8, 128), F32),
        ),
        scratch_shapes=[
            pltpu.VMEM((rows, depth), BF16),
            pltpu.VMEM((rows, wide), BF16),
        ],
        cost_estimate=pl.CostEstimate(
            flops=2 * rows * depth * wide,
            bytes_accessed=2 * (rows * depth + wide * depth + rows * wide),
            transcendentals=0,
        ),
        compiler_params=pltpu.CompilerParams(vmem_limit_bytes=16 * 2**20),
        name="weight_times",
    )(*blocks, *inputs)


def on_device(layer_inputs, projection, pre_act, act_grad):
    weight = projection[0]
    rows = pre_act.shape[1]
    half = rows // 2
    middle = pre_act.shape[2] // 2
    wide = weight.shape[0]

    beneath = along_z(layer_inputs[0], 1)

    own = (
        2.0 * jnp.maximum(pre_act[0].astype(F32), 0.0) * act_grad[0].astype(F32)
    ).astype(BF16)

    left = shift(own, "dp", 2)
    right = shift(own, "dp", -2)
    beside = swap(own, "dp")
    held = jnp.concatenate([layer_inputs[0], beneath])
    near = along_z(held, 2)
    last = along_z(held, -2)
    left, right, beside = together((left, right, beside))

    from_left = shift(jnp.concatenate([left[:half], beside[:half]]), "dp", 2)
    from_right = shift(jnp.concatenate([right[half:], beside[:half]]), "dp", -2)
    from_beside = swap(jnp.concatenate([left[half:], right[half:]]), "dp")

    first_part = times(jnp.concatenate([own, beside, right, left]), weight)
    last, first_part = together((last, first_part))
    beyond = along_z(last, -2)

    from_left, from_right, from_beside, near, beyond = together(
        (from_left, from_right, from_beside, near, beyond)
    )
    across = jnp.concatenate([from_left[:half], from_right[:half]])
    left_beside = jnp.concatenate([from_left[half:], from_beside[:half]])
    right_beside = jnp.concatenate([from_right[half:], from_beside[half:]])
    far_left = shift(left_beside[:, :middle], "dp", 2)
    far_right = shift(right_beside[:, middle:], "dp", -2)

    second_part = times(jnp.concatenate([right_beside, across, left_beside]), weight)
    held, second_part = together((held, second_part))
    held_away = swap(jnp.concatenate([held, near]), "tensor")

    terms = all_terms(first_part, second_part, far_left, far_right, weight)
    beyond, terms = together((beyond, terms))
    beyond_away = swap(jnp.concatenate([beyond, last]), "tensor")

    def term(step):
        begin = step % Z * rows
        return terms[begin : begin + rows].astype(F32)

    def along(total, direction):
        return shift(total.astype(BF16), "tensor", 2 * direction)

    def both(same, away):
        return jnp.concatenate([same, away])

    up, down = along(term(4)[:half], 1), along(term(4)[half:], -1)
    up, down = together((up, down))

    up, down = up.astype(F32), down.astype(F32)
    up = both(term(3)[:half] + up, term(3)[half:])
    down = both(term(-3)[:half], term(-3)[half:] + down)
    up, down = along(up, 1), along(down, -1)
    held_away, own_term = together((held_away, term(0).astype(BF16)))
    pieces = [deliver(own_term[:half], 0, 0), deliver(own_term[half:], 0, 1)]
    up, down, beyond_away = together((up, down, beyond_away))

    up = along(term(2) + up.astype(F32), 1)
    down = along(term(-2) + down.astype(F32), -1)
    weight_grad, zeros = weight_times(
        (own, beside, right, left, from_left, from_right, from_beside, far_left, far_right),
        (held, near, beyond, last, held_away, beyond_away),
    )
    up, down, zeros, *pieces = together((up, down, zeros, *pieces))
    up, down = up.astype(F32) + zeros[:1, :1], down.astype(F32)

    for total, dz in ((term(1) + up, 1), (term(-1) + down, -1)):
        total = total.astype(BF16)
        pieces += [deliver(total[:half], dz, 0), deliver(total[half:], dz, 1)]
    handed = sum(piece.astype(F32) for piece in pieces).astype(BF16)
    return (weight_grad[None], handed[None])


def solution(mesh):
    return jax.shard_map(
        on_device,
        mesh=mesh,
        in_specs=(
            P("section", "tensor", "dp"),
            P("section", "dp", "tensor"),
            P("section", "dp", "tensor"),
            P("section", "dp", "tensor"),
        ),
        out_specs=(P("section", "dp", "tensor"), P("section", "tensor", "dp")),
        check_vma=False,
    )
```

```python
import jax
import jax.numpy as jnp
from jax import lax
from jax.experimental import pallas as pl
from jax.experimental.pallas import tpu as pltpu
from jax.sharding import PartitionSpec as P

F32, BF16 = jnp.float32, jnp.bfloat16
Z, DP, T, S = 8, 8, 16, 2
together = lax.optimization_barrier
OVER_LAST = (((1,), (1,)), ((), ()))


def shift(block, axis, distance):
    n = lax.axis_size(axis)
    return lax.ppermute(block, axis, [(i, (i + distance) % n) for i in range(n)])


def swap(block, axis):
    n = lax.axis_size(axis)
    return lax.ppermute(block, axis, [(i, i ^ 1) for i in range(n)])


def along_z(blocks, distance):
    route = []
    for s in range(S):
        for t in range(T):
            to = (t + 2 * (distance if s == 0 else -distance)) % T
            route.append((s * T + t, s * T + to))
    return lax.ppermute(blocks, ("section", "tensor"), route)


def deliver(block, dz, flip):
    route = []
    for s in range(S):
        for t in range(T):
            to = ((t // 2 + dz) % Z) * 2 + (t % 2 ^ flip)
            route.append((s * T + t, (1 - s) * T + to))
    return lax.ppermute(block, ("section", "tensor"), route)


def times_kernel(block_ref, weight_ref, out_ref):
    wide = weight_ref.shape[0]
    for start in range(0, wide, 256):
        stop = min(start + 256, wide)
        out_ref[:, start:stop] = lax.dot_general(
            block_ref[...],
            weight_ref[start:stop, :],
            (((1,), (1,)), ((), ())),
            preferred_element_type=F32,
        ).astype(out_ref.dtype)


def times(block, weight):
    rows, depth = block.shape
    wide = weight.shape[0]
    return pl.pallas_call(
        times_kernel,
        in_specs=[pl.BlockSpec(memory_space=pltpu.VMEM)] * 2,
        out_specs=pl.BlockSpec(memory_space=pltpu.VMEM),
        out_shape=jax.ShapeDtypeStruct((rows, wide), BF16),
        cost_estimate=pl.CostEstimate(
            flops=2 * rows * depth * wide,
            bytes_accessed=2 * (rows * depth + wide * depth + rows * wide),
            transcendentals=0,
        ),
        compiler_params=pltpu.CompilerParams(vmem_limit_bytes=8 * 2**20),
        name="times",
    )(block, weight)


def place(dx, dy):
    dp = lax.axis_index("dp")
    return ((dp // 2 + dx) % 4) * 2 + (dp % 2 + dy) % 2


FIRST = ((0, 0), (0, 1), (1, 0), (3, 0))
SECOND = ((1, 1), (2, 0), (3, 1))
FAR = ((2, 1),)


def far_kernel(first_ref, second_ref, left_ref, right_ref, weight_ref, out_ref):
    tensor = lax.axis_index("tensor")
    z, y_hi = tensor // 2, tensor % 2
    rows, middle = left_ref.shape
    half = rows // 2

    def fill(which, source, index, columns=slice(None)):
        block = ((place(*which) - z + Z) % Z) * rows
        for high in range(2):
            away = y_hi if high == 0 else 1 - y_hi
            where = pl.multiple_of(block + away * half, half)
            begin = index * rows + high * half
            out_ref[pl.ds(where, half), columns] = source[begin : begin + half, :]

    for i, which in enumerate(FIRST):
        fill(which, first_ref, i)
    for i, which in enumerate(SECOND):
        fill(which, second_ref, i)
    wide = weight_ref.shape[0]
    for start in range(0, wide, 256):
        some = slice(start, min(start + 256, wide))
        total = lax.dot_general(
            left_ref[...], weight_ref[some, :middle], OVER_LAST, preferred_element_type=F32
        )
        total += lax.dot_general(
            right_ref[...], weight_ref[some, middle:], OVER_LAST, preferred_element_type=F32
        )
        fill(FAR[0], total.astype(out_ref.dtype), 0, some)


def all_terms(first, second, left, right, weight):
    rows, middle = left.shape
    wide = weight.shape[0]
    return pl.pallas_call(
        far_kernel,
        in_specs=[pl.BlockSpec(memory_space=pltpu.VMEM)] * 5,
        out_specs=pl.BlockSpec(memory_space=pltpu.VMEM),
        out_shape=jax.ShapeDtypeStruct((DP * rows, wide), BF16),
        cost_estimate=pl.CostEstimate(
            flops=4 * rows * middle * wide,
            bytes_accessed=2 * (2 * rows * middle + 2 * wide * middle + 2 * DP * rows * wide),
            transcendentals=0,
        ),
        compiler_params=pltpu.CompilerParams(vmem_limit_bytes=8 * 2**20),
        name="all_terms",
    )(first, second, left, right, weight)


def weight_kernel(*refs):
    blocks, pieces = refs[:9], refs[9:16]
    out_ref, grads, inputs = refs[16:]
    own, beside, right, left, from_left, from_right, from_beside, far_left, far_right = blocks
    half = own.shape[0] // 2
    middle = far_left.shape[1]
    step = out_ref.shape[0]

    @pl.when(pl.program_id(0) == 0)
    def _():
        tensor, section = lax.axis_index("tensor"), lax.axis_index("section")
        z, y_hi = tensor // 2, tensor % 2

        def fill(spot, high, source, part, columns=slice(None)):
            apart = z - place(*(FIRST + SECOND + FAR)[spot])
            order = (apart * (1 - 2 * section) + Z) % Z
            order ^= order // 4 * 2
            away = y_hi if high == 0 else 1 - y_hi
            where = pl.multiple_of((order + away * Z) * half, half)
            grads[pl.ds(where, half), columns] = source[part * half : (part + 1) * half, :]

        for spot, block in enumerate((own, beside, right, left)):
            fill(spot, 0, block, 0)
            fill(spot, 1, block, 1)
        fill(4, 0, from_right, 1)
        fill(4, 1, from_beside, 1)
        fill(5, 0, from_left, 0)
        fill(5, 1, from_right, 0)
        fill(6, 0, from_left, 1)
        fill(6, 1, from_beside, 0)
        for block, columns in ((far_left, slice(0, middle)), (far_right, slice(middle, None))):
            fill(7, 0, block, 0, columns)
            fill(7, 1, block, 1, columns)
        start = 0
        for block in pieces:
            inputs[start : start + block.shape[0], :] = block[...]
            start += block.shape[0]

    columns = pl.ds(pl.multiple_of(pl.program_id(0) * step, step), step)
    part = inputs[:, columns].T
    wide = grads.shape[1]
    for start in range(0, wide, wide // 3):
        some = slice(start, start + wide // 3)
        out_ref[:, some] = jnp.dot(
            part, grads[:, some], preferred_element_type=F32
        ).astype(out_ref.dtype)


def weight_times(blocks, inputs):
    rows, depth = 8 * blocks[0].shape[0], blocks[0].shape[1]
    wide = inputs[0].shape[1]
    step = wide // 3
    return pl.pallas_call(
        weight_kernel,
        grid=(wide // step,),
        in_specs=[pl.BlockSpec(memory_space=pltpu.VMEM)] * (len(blocks) + len(inputs)),
        out_specs=pl.BlockSpec((step, depth), lambda i: (i, 0)),
        out_shape=jax.ShapeDtypeStruct((wide, depth), BF16),
        scratch_shapes=[
            pltpu.VMEM((rows, depth), BF16),
            pltpu.VMEM((rows, wide), BF16),
        ],
        cost_estimate=pl.CostEstimate(
            flops=2 * rows * depth * wide,
            bytes_accessed=2 * (rows * depth + wide * depth + rows * wide),
            transcendentals=0,
        ),
        compiler_params=pltpu.CompilerParams(vmem_limit_bytes=16 * 2**20),
        name="weight_times",
    )(*blocks, *inputs)


def on_device(layer_inputs, projection, pre_act, act_grad):
    weight = projection[0]
    rows = pre_act.shape[1]
    half = rows // 2
    middle = pre_act.shape[2] // 2
    wide = weight.shape[0]

    beneath = along_z(layer_inputs[0], 1)

    own = (
        2.0 * jnp.maximum(pre_act[0].astype(F32), 0.0) * act_grad[0].astype(F32)
    ).astype(BF16)

    left = shift(own, "dp", 2)
    right = shift(own, "dp", -2)
    beside = swap(own, "dp")
    held = jnp.concatenate([layer_inputs[0], beneath])
    near = along_z(held, 2)
    last = along_z(held, -2)
    left, right, beside = together((left, right, beside))

    from_left = shift(jnp.concatenate([left[:half], beside[:half]]), "dp", 2)
    from_right = shift(jnp.concatenate([right[half:], beside[:half]]), "dp", -2)
    from_beside = swap(jnp.concatenate([left[half:], right[half:]]), "dp")

    first_part = times(jnp.concatenate([own, beside, right, left]), weight)
    last, first_part = together((last, first_part))
    beyond = along_z(last, -2)

    from_left, from_right, from_beside, near = together(
        (from_left, from_right, from_beside, near)
    )
    across = jnp.concatenate([from_left[:half], from_right[:half]])
    left_beside = jnp.concatenate([from_left[half:], from_beside[:half]])
    right_beside = jnp.concatenate([from_right[half:], from_beside[half:]])
    far_left = shift(left_beside[:, :middle], "dp", 2)
    far_right = shift(right_beside[:, middle:], "dp", -2)

    second = jnp.concatenate([right_beside, across, left_beside])
    second, beyond = together((second, beyond))
    second_part = times(second, weight)
    held, second_part = together((held, second_part))
    held_away = swap(held, "tensor")

    terms = all_terms(first_part, second_part, far_left, far_right, weight)
    near, terms = together((near, terms))
    middle_away = swap(jnp.concatenate([near, last]), "tensor")

    def term(step):
        begin = step % Z * rows
        return terms[begin : begin + rows].astype(F32)

    def along(total, direction):
        return shift(total.astype(BF16), "tensor", 2 * direction)

    def both(same, away):
        return jnp.concatenate([same, away])

    up, down = along(term(4)[:half], 1), along(term(4)[half:], -1)
    up, down, held_away, beyond, own_term = together(
        (up, down, held_away, beyond, term(0).astype(BF16))
    )
    beyond_away = swap(beyond, "tensor")

    up, down = up.astype(F32), down.astype(F32)
    up = both(term(3)[:half] + up, term(3)[half:])
    down = both(term(-3)[:half], term(-3)[half:] + down)
    up, down = along(up, 1), along(down, -1)
    pieces = [deliver(own_term[:half], 0, 0), deliver(own_term[half:], 0, 1)]
    up, down, middle_away = together((up, down, middle_away))

    up, down = term(2) + up.astype(F32), term(-2) + down.astype(F32)
    parts = [(along(up[half:], 1), 1, half, 1), (along(down[half:], -1), -1, half, 1)]
    parts += [(along(up[:half], 1), 1, 0, 0), (along(down[:half], -1), -1, 0, 0)]
    arrived, *pieces = together((parts[0][0], *pieces))
    parts[0] = (arrived, *parts[0][1:])
    for part, dz, low, flip in parts:
        total = term(dz)[low : low + half] + part.astype(F32)
        pieces.append(deliver(total.astype(BF16), dz, flip))
    handed = sum(piece.astype(F32) for piece in pieces).astype(BF16)
    weight_grad = weight_times(
        (own, beside, right, left, from_left, from_right, from_beside, far_left, far_right),
        (held, near, last, beyond, held_away, middle_away, beyond_away),
    )
    return (weight_grad[None], handed[None])


def solution(mesh):
    return jax.shard_map(
        on_device,
        mesh=mesh,
        in_specs=(
            P("section", "tensor", "dp"),
            P("section", "dp", "tensor"),
            P("section", "dp", "tensor"),
            P("section", "dp", "tensor"),
        ),
        out_specs=(P("section", "dp", "tensor"), P("section", "tensor", "dp")),
        check_vma=False,
    )
```

```python
import jax
import jax.numpy as jnp
from jax import lax
from jax.experimental import pallas as pl
from jax.experimental.pallas import tpu as pltpu
from jax.sharding import PartitionSpec as P

F32, BF16 = jnp.float32, jnp.bfloat16
Z, DP, T, S = 8, 8, 16, 2
together = lax.optimization_barrier
OVER_LAST = (((1,), (1,)), ((), ()))


def shift(block, axis, distance):
    n = lax.axis_size(axis)
    return lax.ppermute(block, axis, [(i, (i + distance) % n) for i in range(n)])


def swap(block, axis):
    n = lax.axis_size(axis)
    return lax.ppermute(block, axis, [(i, i ^ 1) for i in range(n)])


def along_z(blocks, distance):
    route = []
    for s in range(S):
        for t in range(T):
            to = (t + 2 * (distance if s == 0 else -distance)) % T
            route.append((s * T + t, s * T + to))
    return lax.ppermute(blocks, ("section", "tensor"), route)


def deliver(block, dz, flip):
    route = []
    for s in range(S):
        for t in range(T):
            to = ((t // 2 + dz) % Z) * 2 + (t % 2 ^ flip)
            route.append((s * T + t, (1 - s) * T + to))
    return lax.ppermute(block, ("section", "tensor"), route)


def times_kernel(block_ref, weight_ref, out_ref):
    wide = weight_ref.shape[0]
    for start in range(0, wide, 256):
        stop = min(start + 256, wide)
        out_ref[:, start:stop] = lax.dot_general(
            block_ref[...],
            weight_ref[start:stop, :],
            (((1,), (1,)), ((), ())),
            preferred_element_type=F32,
        ).astype(out_ref.dtype)


def times(block, weight):
    rows, depth = block.shape
    wide = weight.shape[0]
    return pl.pallas_call(
        times_kernel,
        in_specs=[pl.BlockSpec(memory_space=pltpu.VMEM)] * 2,
        out_specs=pl.BlockSpec(memory_space=pltpu.VMEM),
        out_shape=jax.ShapeDtypeStruct((rows, wide), BF16),
        cost_estimate=pl.CostEstimate(
            flops=2 * rows * depth * wide,
            bytes_accessed=2 * (rows * depth + wide * depth + rows * wide),
            transcendentals=0,
        ),
        compiler_params=pltpu.CompilerParams(vmem_limit_bytes=8 * 2**20),
        name="times",
    )(block, weight)


def place(dx, dy):
    dp = lax.axis_index("dp")
    return ((dp // 2 + dx) % 4) * 2 + (dp % 2 + dy) % 2


FIRST = ((0, 0), (0, 1), (1, 0), (3, 0))
SECOND = ((1, 1), (2, 0), (3, 1))
FAR = ((2, 1),)


def far_kernel(first_ref, second_ref, left_ref, right_ref, weight_ref, out_ref):
    tensor = lax.axis_index("tensor")
    z, y_hi = tensor // 2, tensor % 2
    rows, middle = left_ref.shape
    half = rows // 2

    def fill(which, source, index, columns=slice(None)):
        block = ((place(*which) - z + Z) % Z) * rows
        for high in range(2):
            away = y_hi if high == 0 else 1 - y_hi
            where = pl.multiple_of(block + away * half, half)
            begin = index * rows + high * half
            out_ref[pl.ds(where, half), columns] = source[begin : begin + half, :]

    for i, which in enumerate(FIRST):
        fill(which, first_ref, i)
    for i, which in enumerate(SECOND):
        fill(which, second_ref, i)
    wide = weight_ref.shape[0]
    for start in range(0, wide, 256):
        some = slice(start, min(start + 256, wide))
        total = lax.dot_general(
            left_ref[...], weight_ref[some, :middle], OVER_LAST, preferred_element_type=F32
        )
        total += lax.dot_general(
            right_ref[...], weight_ref[some, middle:], OVER_LAST, preferred_element_type=F32
        )
        fill(FAR[0], total.astype(out_ref.dtype), 0, some)


def all_terms(first, second, left, right, weight):
    rows, middle = left.shape
    wide = weight.shape[0]
    return pl.pallas_call(
        far_kernel,
        in_specs=[pl.BlockSpec(memory_space=pltpu.VMEM)] * 5,
        out_specs=pl.BlockSpec(memory_space=pltpu.VMEM),
        out_shape=jax.ShapeDtypeStruct((DP * rows, wide), BF16),
        cost_estimate=pl.CostEstimate(
            flops=4 * rows * middle * wide,
            bytes_accessed=2 * (2 * rows * middle + 2 * wide * middle + 2 * DP * rows * wide),
            transcendentals=0,
        ),
        compiler_params=pltpu.CompilerParams(vmem_limit_bytes=8 * 2**20),
        name="all_terms",
    )(first, second, left, right, weight)


def weight_kernel(*refs):
    blocks, pieces = refs[:9], refs[9:16]
    out_ref, grads, inputs = refs[16:]
    own, beside, right, left, from_left, from_right, from_beside, far_left, far_right = blocks
    half = own.shape[0] // 2
    middle = far_left.shape[1]
    step = out_ref.shape[0]

    @pl.when(pl.program_id(0) == 0)
    def _():
        tensor, section = lax.axis_index("tensor"), lax.axis_index("section")
        z, y_hi = tensor // 2, tensor % 2

        def fill(spot, high, source, part, columns=slice(None)):
            apart = z - place(*(FIRST + SECOND + FAR)[spot])
            order = (apart * (1 - 2 * section) + Z) % Z
            order ^= order // 4 * 2
            away = y_hi if high == 0 else 1 - y_hi
            where = pl.multiple_of((order + away * Z) * half, half)
            grads[pl.ds(where, half), columns] = source[part * half : (part + 1) * half, :]

        for spot, block in enumerate((own, beside, right, left)):
            fill(spot, 0, block, 0)
            fill(spot, 1, block, 1)
        fill(4, 0, from_right, 1)
        fill(4, 1, from_beside, 1)
        fill(5, 0, from_left, 0)
        fill(5, 1, from_right, 0)
        fill(6, 0, from_left, 1)
        fill(6, 1, from_beside, 0)
        for block, columns in ((far_left, slice(0, middle)), (far_right, slice(middle, None))):
            fill(7, 0, block, 0, columns)
            fill(7, 1, block, 1, columns)
        start = 0
        for block in pieces:
            inputs[start : start + block.shape[0], :] = block[...]
            start += block.shape[0]

    columns = pl.ds(pl.multiple_of(pl.program_id(0) * step, step), step)
    part = inputs[:, columns].T
    wide = grads.shape[1]
    for start in range(0, wide, wide // 3):
        some = slice(start, start + wide // 3)
        out_ref[:, some] = jnp.dot(
            part, grads[:, some], preferred_element_type=F32
        ).astype(out_ref.dtype)


def weight_times(blocks, inputs):
    rows, depth = 8 * blocks[0].shape[0], blocks[0].shape[1]
    wide = inputs[0].shape[1]
    step = wide // 3
    return pl.pallas_call(
        weight_kernel,
        grid=(wide // step,),
        in_specs=[pl.BlockSpec(memory_space=pltpu.VMEM)] * (len(blocks) + len(inputs)),
        out_specs=pl.BlockSpec((step, depth), lambda i: (i, 0)),
        out_shape=jax.ShapeDtypeStruct((wide, depth), BF16),
        scratch_shapes=[
            pltpu.VMEM((rows, depth), BF16),
            pltpu.VMEM((rows, wide), BF16),
        ],
        cost_estimate=pl.CostEstimate(
            flops=2 * rows * depth * wide,
            bytes_accessed=2 * (rows * depth + wide * depth + rows * wide),
            transcendentals=0,
        ),
        compiler_params=pltpu.CompilerParams(vmem_limit_bytes=16 * 2**20),
        name="weight_times",
    )(*blocks, *inputs)


def on_device(layer_inputs, projection, pre_act, act_grad):
    weight = projection[0]
    rows = pre_act.shape[1]
    half = rows // 2
    middle = pre_act.shape[2] // 2
    wide = weight.shape[0]

    beneath = along_z(layer_inputs[0], 1)

    own = (
        2.0 * jnp.maximum(pre_act[0].astype(F32), 0.0) * act_grad[0].astype(F32)
    ).astype(BF16)

    left = shift(own, "dp", 2)
    right = shift(own, "dp", -2)
    beside = swap(own, "dp")
    held = jnp.concatenate([layer_inputs[0], beneath])
    near = along_z(held, 2)
    last = along_z(held, -2)
    left, right, beside = together((left, right, beside))

    from_left = shift(jnp.concatenate([left[:half], beside[:half]]), "dp", 2)
    from_right = shift(jnp.concatenate([right[half:], beside[:half]]), "dp", -2)
    from_beside = swap(jnp.concatenate([left[half:], right[half:]]), "dp")

    first_part = times(jnp.concatenate([own, beside, right, left]), weight)
    last, first_part = together((last, first_part))
    beyond = along_z(last, -2)

    from_left, from_right, from_beside, near = together(
        (from_left, from_right, from_beside, near)
    )
    across = jnp.concatenate([from_left[:half], from_right[:half]])
    left_beside = jnp.concatenate([from_left[half:], from_beside[:half]])
    right_beside = jnp.concatenate([from_right[half:], from_beside[half:]])
    far_left = shift(left_beside[:, :middle], "dp", 2)
    far_right = shift(right_beside[:, middle:], "dp", -2)

    second = jnp.concatenate([right_beside, across, left_beside])
    second, beyond = together((second, beyond))
    second_part = times(second, weight)
    held, second_part = together((held, second_part))
    held_away = swap(held, "tensor")

    terms = all_terms(first_part, second_part, far_left, far_right, weight)
    near, terms = together((near, terms))
    middle_away = swap(jnp.concatenate([near, last]), "tensor")

    def term(step):
        begin = step % Z * rows
        return terms[begin : begin + rows].astype(F32)

    def along(total, direction):
        return shift(total.astype(BF16), "tensor", 2 * direction)

    def half_of(step, low, part=0.0):
        return term(step)[low : low + half] + part

    up_same, down_away = along(half_of(4, 0), 1), along(half_of(4, half), -1)
    up_away, down_same = along(half_of(3, half), 1), along(half_of(-3, 0), -1)
    up_same, down_away, up_away, down_same, held_away = together(
        (up_same, down_away, up_away, down_same, held_away)
    )
    up_away = along(half_of(2, half, up_away.astype(F32)), 1)
    down_same = along(half_of(-2, 0, down_same.astype(F32)), -1)
    up_same = along(half_of(3, 0, up_same.astype(F32)), 1)
    down_away = along(half_of(-3, half, down_away.astype(F32)), -1)
    up_away, down_same, up_same, down_away, middle_away, beyond, own_term = together(
        (up_away, down_same, up_same, down_away, middle_away, beyond, term(0).astype(BF16))
    )
    up_same = along(half_of(2, 0, up_same.astype(F32)), 1)
    down_away = along(half_of(-2, half, down_away.astype(F32)), -1)
    beyond_away = swap(beyond, "tensor")
    pieces = [deliver(own_term[:half], 0, 0), deliver(own_term[half:], 0, 1)]
    for part, dz, low, flip in (
        (up_away, 1, half, 1),
        (down_same, -1, 0, 0),
        (up_same, 1, 0, 0),
        (down_away, -1, half, 1),
    ):
        total = half_of(dz, low, part.astype(F32))
        pieces.append(deliver(total.astype(BF16), dz, flip))
    handed = sum(piece.astype(F32) for piece in pieces).astype(BF16)
    weight_grad = weight_times(
        (own, beside, right, left, from_left, from_right, from_beside, far_left, far_right),
        (held, near, last, beyond, held_away, middle_away, beyond_away),
    )
    return (weight_grad[None], handed[None])


def solution(mesh):
    return jax.shard_map(
        on_device,
        mesh=mesh,
        in_specs=(
            P("section", "tensor", "dp"),
            P("section", "dp", "tensor"),
            P("section", "dp", "tensor"),
            P("section", "dp", "tensor"),
        ),
        out_specs=(P("section", "dp", "tensor"), P("section", "tensor", "dp")),
        check_vma=False,
    )
```
